32 devices in a mesh: sub: 8 (over z, core), hgt: 4 (over y, x).
Axes of the slice: x: 2, y: 2, z: 4, core: 2. Of those that a mesh axis runs over, the one named last changes fastest.
Arguments:
- polar_beams: bfloat16 [4, 2, 128, 4096], P('hgt', None, 'sub'), may hold values from -6 to 6
- band_start: int32 [3, 2, 2, 16], replicated, may hold values from 0 to 8, as said below
- band_weight: bfloat16 [3, 2, 2, 16, 8], replicated, may hold values from -1.5 to 1.5
- phase_rate: float32 [3, 2, 2, 16], replicated, may hold values from -6 to 6
- layer_wave: float32 [4], P('hgt'), may hold values from 0.5 to 2
- beam_map: int32 [16, 2048], replicated, may hold values from 0 to 126, as said below
- range_map: int32 [16, 2048], replicated, may hold values from 0 to 4094
- pixel_frac: bfloat16 [3, 16, 2048], replicated, may hold values from 0 to 1
Outputs:
- image: float32 [16, 4, 2, 2048], P('sub', 'hgt')
The draws below stay inside these ranges and needn't reach their ends.
Inputs may be any that keep to these rules, and one draw needn't show every extreme that they name: band_start[l,k,h,j] + t for t < 8 lies within h * 8 - 8 to h * 8 + 16 / 2 + 7. beam_map[y, x] differs from x * 128 // 2048 by at most 2.
All inputs are finite; a program needn't handle non-finite values.
Results may differ from the reference program's by a relative error of at most 0.0041.
Values may be sent and summed in bfloat16 or wider, within the bound.
A program may use at most 192 MiB of HBM per device.

```python
import math
import jax
import jax.numpy as jnp
import numpy as np
from jax import lax

RANGE = 4096
BEAMS = 16
TAPS = 8
LEVELS = 3
IMG_COLS = 2048
HEIGHTS = 4
TOTAL_BEAMS = 128
IMG_ROWS = 16
MERGED = 128
N_SUB = 8


def draw_band_start(key, part):
    beam_ids = jnp.arange(BEAMS, dtype=jnp.int32)
    halves = jnp.arange(2, dtype=jnp.int32)
    centre = halves[:, None] * (BEAMS // 2) + beam_ids[None, :] // 2 - TAPS // 2
    jitter = jax.random.randint(key, (LEVELS, 2, 2, BEAMS), -1, 2, dtype=jnp.int32)
    return jnp.clip(centre[None, None] + jitter, 0, BEAMS - TAPS).astype(jnp.int32)


def draw_beam_map(key, part):
    merged_count = BEAMS * 2 ** LEVELS
    columns = jnp.arange(IMG_COLS, dtype=jnp.int32)
    centre = columns * merged_count // IMG_COLS
    jitter = jax.random.randint(key, (IMG_ROWS, IMG_COLS), -2, 3, dtype=jnp.int32)
    chosen = jnp.clip(centre[None, :] + jitter, 0, merged_count - 2)
    chosen = chosen.at[0, 0].set(0).at[0, IMG_COLS - 1].set(merged_count - 2)
    return chosen.astype(jnp.int32)


def draw_range_map(key, part):
    chosen = jax.random.randint(key, (IMG_ROWS, IMG_COLS), 0, RANGE - 1, dtype=jnp.int32)
    chosen = chosen.at[0, 0].set(0).at[0, IMG_COLS - 1].set(RANGE - 2)
    return chosen.astype(jnp.int32)


def level_of(stream_key, dims, pieces, smallest, largest):
    factor_of, own = 1.0, jax.random.fold_in(stream_key, 6)
    for dim, parts in pieces:
        heights = jnp.exp(jax.random.uniform(jax.random.fold_in(own, dim), (parts,), jnp.float32, smallest / len(pieces), largest / len(pieces)))
        factor_of = factor_of * jnp.repeat(heights, dims[dim] // parts).reshape([-1 if axis == dim else 1 for axis in range(len(dims))])
    return factor_of


def bell_draw(rng, shape, scale, limit, pieces=(), kind=jnp.bfloat16):
    entries = jax.random.normal(rng, shape, jnp.float32) * scale
    if len(pieces) > 0:
        entries = level_of(rng, shape, pieces, -0.22, 0.18) * entries
    return jnp.clip(entries, min=-limit, max=limit).astype(kind)


def setup_inputs(seed: int = 0) -> dict:
    streams_of = jax.random.split(jax.random.key(seed), 9)
    polar_beams = bell_draw(streams_of[0], (HEIGHTS, 2, TOTAL_BEAMS, RANGE), 1.0, 6.0, ((0, 4), (2, 8)))
    band_start = draw_band_start(jax.random.fold_in(streams_of[8], 71), 0)
    band_weight = bell_draw(streams_of[2], (LEVELS, 2, 2, BEAMS, TAPS), 0.25, 1.5)
    phase_rate = jnp.clip(jax.random.uniform(streams_of[3], (LEVELS, 2, 2, BEAMS), jnp.float32, -6.0, 6.0), -6.0, 6.0)
    layer_wave = jnp.clip(jnp.exp(math.log(2.0) - 1.3862944 * jax.random.uniform(streams_of[4], (HEIGHTS,), jnp.float32) ** level_of(streams_of[4], (HEIGHTS,), ((0, 4),), -0.2, 0.2)), 0.5, 2.0)
    beam_map = draw_beam_map(jax.random.fold_in(streams_of[8], 71), 0)
    range_map = draw_range_map(jax.random.fold_in(streams_of[8], 71), 0)
    pixel_frac = jnp.clip(jax.random.uniform(streams_of[7], (3, IMG_ROWS, IMG_COLS), jnp.float32, 0.0, 1.0), 0.0, 1.0).astype(jnp.bfloat16)
    return dict(polar_beams=polar_beams, band_start=band_start, band_weight=band_weight, phase_rate=phase_rate, layer_wave=layer_wave, beam_map=beam_map, range_map=range_map, pixel_frac=pixel_frac)


range_phase = 0.003


def rotate(real_part, imag_part, angles):
    cosine = jnp.cos(angles)
    sine_part = jnp.sin(angles)
    return cosine * real_part - sine_part * imag_part, sine_part * real_part + cosine * imag_part


def reverse_bits(value, width):
    result = 0
    for bit_idx in range(width):
        result = result * 2 + ((value >> bit_idx) & 1)
    return result


def band_apply(values, starts, weights):
    accumulated = jnp.zeros(values.shape[:3] + (BEAMS, RANGE), jnp.float32)
    for tap_idx in range(TAPS):
        accumulated = accumulated + weights[:, tap_idx][:, None] * jnp.take(values, (starts + tap_idx).astype(jnp.int32), axis=3)
    return accumulated


def reference(polar_beams, band_start, band_weight, phase_rate, layer_wave, beam_map, range_map, pixel_frac):
    range_pos = (jnp.arange(RANGE, dtype=jnp.float32) + 0.5) / RANGE
    beam_frac = pixel_frac[0].astype(jnp.float32)
    range_fr = pixel_frac[1].astype(jnp.float32)
    height_frac = pixel_frac[2].astype(jnp.float32)
    groups = N_SUB // 2 ** LEVELS
    sector_device = np.array([reverse_bits(sector, LEVELS) for sector in range(2 ** LEVELS)], dtype=np.int32)

    def merge_section(current, section, wavenumber):
        values = current.astype(jnp.float32).reshape(2, N_SUB // 2 ** (section + 1), 2, 2 ** section, BEAMS, RANGE)
        halves = []
        for my_half in range(2):
            summed = None
            for child in range(2):
                shifted = band_apply(values[:, :, child], band_start[section, child, my_half], band_weight[section, child, my_half].astype(jnp.float32))
                angles = wavenumber * phase_rate[section, child, my_half][:, None] * range_pos[None, :]
                real_part, imag_part = rotate(shifted[0], shifted[1], angles[None, None])
                term = jnp.stack([real_part, imag_part])
                summed = term if child == 0 else summed + term
            halves.append(summed)
        return jnp.stack(halves, axis=2).reshape(2, N_SUB, BEAMS, RANGE)

    def one_layer(inputs):
        layer_beams, wavenumber = inputs
        current = layer_beams.reshape(2, N_SUB, BEAMS, RANGE)
        for section in range(LEVELS):
            merged_out = merge_section(current, section, wavenumber)
            current = merged_out.astype(jnp.bfloat16) if section + 1 < LEVELS else merged_out
        ordered = current.reshape(2, groups, 2 ** LEVELS, BEAMS, RANGE)[:, :, sector_device]
        flat_polar = ordered.reshape(2, groups, MERGED * RANGE)
        summed = jnp.zeros((2, IMG_ROWS, IMG_COLS), jnp.float32)
        for beam_step in range(2):
            beam_part = beam_frac if beam_step else 1.0 - beam_frac
            for range_step in range(2):
                pair_weight = beam_part * (range_fr if range_step else 1.0 - range_fr)
                flat_index = ((beam_map + beam_step) * RANGE + range_map + range_step).reshape(-1).astype(jnp.int32)
                sampled = jnp.sum(jnp.take(flat_polar, flat_index, axis=2), axis=1).reshape(2, IMG_ROWS, IMG_COLS)
                summed = summed + pair_weight[None] * sampled
        angles = wavenumber * range_phase * (range_map.astype(jnp.float32) + range_fr)
        real_part, imag_part = rotate(summed[0], summed[1], angles)
        return jnp.stack([real_part, imag_part])

    cart = lax.map(one_layer, (polar_beams, layer_wave))
    upper_layers = jnp.concatenate([cart[1:], jnp.zeros_like(cart[:1])], axis=0)
    blended = (1.0 - height_frac)[None, None] * cart + height_frac[None, None] * upper_layers
    return jnp.transpose(blended, (2, 0, 1, 3))
```

```python
import functools

import jax
import jax.numpy as jnp
from jax import lax
from jax.experimental import pallas as pl
from jax.experimental.pallas import tpu as pltpu
from jax.sharding import PartitionSpec as P

range_phase = 0.003
LANES = 128
SLOT = 256
MESH = pl.DeviceIdType.MESH
VMEM = pltpu.VMEM


def sincos(x):
    q = jnp.floor(x * 0.6366197723675814 + 0.5)
    y = x - q * 1.5703125
    y = y - q * 4.837512969970703e-4
    y = y - q * 7.549789948768648e-8
    z = y * y
    s = y + y * z * (-1.6666654611e-1 + z * (8.3321608736e-3 + z * -1.9515295891e-4))
    c = 1.0 - 0.5 * z + z * z * (
        4.166664568298827e-2 + z * (-1.388731625493765e-3 + z * 2.443315711809948e-5)
    )
    n = q.astype(jnp.int32)
    odd = (n & 1) == 1
    sin_ = jnp.where(odd, c, s)
    cos_ = jnp.where(odd, s, c)
    sin_ = jnp.where((n & 2) == 2, -sin_, sin_)
    cos_ = jnp.where(((n + 1) & 2) == 2, -cos_, cos_)
    return sin_, cos_


def reverse_bits(value, width):
    result = 0
    for bit in range(width):
        result = result * 2 + ((value >> bit) & 1)
    return result


def iota(shape, dim):
    return lax.broadcasted_iota(jnp.int32, shape, dim)


def spread(out_ref, values):
    for y in range(values.shape[0]):
        out_ref[y] = values[y : y + 1].astype(out_ref.dtype)


def column_of(row, size):
    eye = iota((size, size), 0) == iota((size, size), 1)
    return jnp.sum(jnp.where(eye, row, 0.0), axis=1, keepdims=True)


def exchange_kernel(group, polar_ref, out_ref, send_sem, recv_sem, own_sem):
    me = lax.axis_index("sub")
    place = lax.rem(me, group)
    base = me - place
    chunk = out_ref.shape[-1]

    def columns(index):
        return pl.ds(pl.multiple_of(index * chunk, chunk), chunk)

    barrier = pltpu.get_barrier_semaphore()
    for i in range(1, group):
        pl.semaphore_signal(
            barrier, inc=1, device_id={"sub": base + lax.rem(place + i, group)}, device_id_type=MESH
        )
    pl.semaphore_wait(barrier, group - 1)
    own = pltpu.make_async_copy(polar_ref.at[0, :, :, columns(place)], out_ref.at[place], own_sem)
    copies = []
    for i in range(1, group):
        there = lax.rem(place + i, group)
        copies.append(
            pltpu.make_async_remote_copy(
                src_ref=polar_ref.at[0, :, :, columns(there)],
                dst_ref=out_ref.at[place],
                send_sem=send_sem.at[i],
                recv_sem=recv_sem.at[i],
                device_id={"sub": base + there},
                device_id_type=MESH,
            )
        )
        copies[-1].start()
    own.start()
    own.wait()
    for copy in copies:
        copy.wait()


def tables(levels, beams, first, total, wave, start_ref, weight_ref, rate_ref, m_ref, cos_ref, sin_ref):
    group = 2**levels
    width = group * beams
    chunk = cos_ref.shape[-1]
    lane = iota((beams, width), 1)
    lane_beam = (lane % beams).astype(jnp.float32)
    lane_sub = lane // beams
    pos = (iota((1, chunk), 1).astype(jnp.float32) + first + 0.5) / total
    for l in range(levels):
        for k in range(2):
            for h in range(2):
                start = column_of(start_ref[l, k, h : h + 1].astype(jnp.float32), beams)
                weight = weight_ref[l, k, h].astype(jnp.float32)
                band = jnp.zeros((beams, width), jnp.float32)
                for t in range(weight.shape[1]):
                    band = jnp.where(lane_beam == start + t, weight[:, t : t + 1], band)
                for s in range(group):
                    if (s >> l) & 1 == h:
                        child = (s & ~(1 << l)) | (k << l)
                        m_ref[l, pl.ds((k * group + s) * beams, beams), :] = jnp.where(
                            lane_sub == child, band, 0.0
                        ).astype(jnp.bfloat16)
                rate = column_of(rate_ref[l, k, h : h + 1], beams)
                sine, cosine = sincos(wave * rate * pos)
                cos_ref[l, k, h] = cosine
                sin_ref[l, k, h] = sine


def merge(levels, beams, x_ref, cur_ref, y_ref, m_ref, cos_ref, sin_ref):
    group = 2**levels
    width = group * beams
    chunk = x_ref.shape[-1]
    for s in range(group):
        for c in range(2):
            cur_ref[pl.ds(s * beams, beams), pl.ds(c * chunk, chunk)] = x_ref[s, c]
    for l in range(levels):
        y_ref[...] = jnp.dot(m_ref[l], cur_ref[...], preferred_element_type=jnp.float32)
        for s in range(group):
            h = (s >> l) & 1
            real = imag = 0.0
            for k in range(2):
                rows = pl.ds((k * group + s) * beams, beams)
                yr = y_ref[rows, pl.ds(0, chunk)]
                yi = y_ref[rows, pl.ds(chunk, chunk)]
                cosine, sine = cos_ref[l, k, h], sin_ref[l, k, h]
                real = real + (cosine * yr - sine * yi)
                imag = imag + (sine * yr + cosine * yi)
            cur_ref[pl.ds(s * beams, beams), pl.ds(0, chunk)] = real.astype(jnp.bfloat16)
            cur_ref[pl.ds(s * beams, beams), pl.ds(chunk, chunk)] = imag.astype(jnp.bfloat16)


def arrange(levels, beams, margin, cur_ref, l_ref, edge_ref):
    group = 2**levels
    width = group * beams
    chunk = cur_ref.shape[1] // 2
    padded = l_ref.shape[3]
    row = iota((padded, width), 0)
    lane = iota((padded, width), 1)
    beam = reverse_bits(lane // beams, levels) * beams + lane % beams
    for e in range(2):
        pick = jnp.where(row - (margin + 8 * e) == beam, 1.0, 0.0).astype(jnp.bfloat16)
        moved = jnp.dot(pick, cur_ref[...], preferred_element_type=jnp.float32)
        for m in range(l_ref.shape[1]):
            for c in range(2):
                part = moved[:, c * chunk + m * SLOT : c * chunk + (m + 1) * SLOT]
                l_ref[e, m, c] = part.astype(jnp.bfloat16)
                edge_ref[e, m, c] = jnp.broadcast_to(part[:, 0:1], (padded, LANES))


def pixels(margin, first, dest, tile_rows, range_ref, beam_ref, f0_ref, f1_ref, l_ref, edge_ref, part_ref):
    columns = range_ref.shape[2]
    slots = l_ref.shape[1]
    lanes_out = part_ref.shape[1]
    blocks = columns // lanes_out
    kappa = iota((SLOT, LANES), 0).astype(jnp.float32).astype(jnp.bfloat16)
    beta = iota((16, LANES), 0)
    for i in range(columns // LANES):
        e = i % 2
        top = 8 * i + 8 * e
        lhs = jnp.concatenate(
            [l_ref[e, m, c, top : top + 16] for m in range(slots) for c in range(2)], axis=0
        )
        edges = [
            jnp.concatenate([edge_ref[e, m, c, top : top + 16] for c in range(2)], axis=0)
            for m in range(slots)
        ]
        cols = slice(i * LANES, (i + 1) * LANES)
        ws, infos = [], []
        for row in range(tile_rows):
            y = dest * tile_rows + row
            u = range_ref[y, :, cols] - first
            f1 = f1_ref[y, :, cols]
            inside = (u >= 0) & (u < slots * SLOT)
            near = jnp.where(inside, u & (SLOT - 1), -8)
            near_b = near.astype(jnp.float32).astype(jnp.bfloat16)
            far_b = (near + 1).astype(jnp.float32).astype(jnp.bfloat16)
            w = jnp.where(
                kappa == near_b,
                (1.0 - f1).astype(jnp.bfloat16),
                jnp.where(kappa == far_b, f1.astype(jnp.bfloat16), jnp.bfloat16(0.0)),
            )
            ws.append(w)
            infos.append((u, f1, y))
        out = jnp.dot(lhs, jnp.concatenate(ws, axis=1), preferred_element_type=jnp.float32)
        for row in range(tile_rows):
            u, f1, y = infos[row]
            mine = out[:, row * LANES : (row + 1) * LANES]
            value = mine[0:32]
            for m in range(1, slots):
                value = jnp.where(u >= m * SLOT, mine[m * 32 : (m + 1) * 32], value)
            for m in range(slots):
                value = value + jnp.where(u == m * SLOT - 1, f1, 0.0) * edges[m]
            f0 = f0_ref[y, :, cols]
            low = beam_ref[y, :, cols] - (8 * i - margin)
            weight = jnp.where(beta == low, 1.0 - f0, jnp.where(beta == low + 1, f0, 0.0))
            lane0 = (i * LANES) % lanes_out
            for c in range(2):
                total = jnp.sum(value[c * 16 : c * 16 + 16] * weight, axis=0, keepdims=True)
                at = c * tile_rows * blocks + row * blocks + (i * LANES) // lanes_out
                part_ref[at : at + 1, lane0 : lane0 + LANES] = total


def compute_kernel(
    levels, margin, total, tile_rows,
    x_ref, start_ref, weight_ref, rate_ref, wave_ref, beam_ref, range_ref, frac_ref,
    out_ref,
    m_ref, cos_ref, sin_ref, cur_ref, y_ref, l_ref, edge_ref, f0_ref, f1_ref, beam3_ref, range3_ref, part_ref,
):
    group = 2**levels
    beams = x_ref.shape[2]
    chunk = x_ref.shape[-1]
    first = lax.rem(lax.axis_index("sub"), group) * chunk
    wave = wave_ref[0]
    tables(
        levels, beams, first.astype(jnp.float32), total, wave,
        start_ref, weight_ref, rate_ref, m_ref, cos_ref, sin_ref,
    )
    spread(f0_ref, frac_ref[0].astype(jnp.float32))
    spread(f1_ref, frac_ref[1].astype(jnp.float32))
    spread(beam3_ref, beam_ref[...])
    spread(range3_ref, range_ref[...])
    merge(levels, beams, x_ref, cur_ref, y_ref, m_ref, cos_ref, sin_ref)
    arrange(levels, beams, margin, cur_ref, l_ref, edge_ref)

    def one(dest, carry):
        pixels(
            margin, first, dest, tile_rows, range3_ref, beam3_ref, f0_ref, f1_ref,
            l_ref, edge_ref, part_ref,
        )
        out_ref[dest] = part_ref[...].astype(jnp.bfloat16)
        return carry

    lax.fori_loop(0, out_ref.shape[0], one, 0)


def finish_kernel(
    tile_rows,
    part_ref, wave_ref, range_ref, frac_ref,
    out_ref,
    got_ref, cart_ref, above_ref, range3_ref, f1_ref, f2_ref, send_sem, recv_sem, layer_send, layer_recv,
):
    me, layer = lax.axis_index("sub"), lax.axis_index("hgt")
    count, layers = lax.axis_size("sub"), lax.axis_size("hgt")
    lanes_out = part_ref.shape[2]
    columns = range_ref.shape[1]
    blocks = columns // lanes_out
    half = tile_rows * blocks
    has_low, has_high = layer > 0, layer < layers - 1

    barrier = pltpu.get_barrier_semaphore()
    for i in range(1, count):
        pl.semaphore_signal(
            barrier, inc=1, device_id={"sub": lax.rem(me + i, count)}, device_id_type=MESH
        )

    @pl.when(has_low)
    def _():
        pl.semaphore_signal(barrier, inc=1, device_id={"hgt": layer - 1}, device_id_type=MESH)

    @pl.when(has_high)
    def _():
        pl.semaphore_signal(barrier, inc=1, device_id={"hgt": layer + 1}, device_id_type=MESH)

    pl.semaphore_wait(barrier, count - 1 + has_low.astype(jnp.int32) + has_high.astype(jnp.int32))
    copies = []
    for i in range(1, count):
        there = lax.rem(me + i, count)
        copies.append(
            pltpu.make_async_remote_copy(
                src_ref=part_ref.at[there],
                dst_ref=got_ref.at[i],
                send_sem=send_sem.at[i],
                recv_sem=recv_sem.at[i],
                device_id={"sub": there},
                device_id_type=MESH,
            )
        )
        copies[-1].start()

    spread(range3_ref, range_ref[...])
    spread(f1_ref, frac_ref[1].astype(jnp.float32))
    spread(f2_ref, frac_ref[2].astype(jnp.float32))

    def dense(ref):
        return jnp.concatenate(
            [
                ref[me * tile_rows + row, :, b * lanes_out : (b + 1) * lanes_out]
                for row in range(tile_rows)
                for b in range(blocks)
            ],
            axis=0,
        )

    angles = wave_ref[0] * range_phase * (dense(range3_ref).astype(jnp.float32) + dense(f1_ref))
    sine, cosine = sincos(angles)
    f2 = dense(f2_ref)
    total = part_ref[me].astype(jnp.float32)
    for i in range(1, count):
        copies[i - 1].wait_recv()
        total = total + got_ref[i].astype(jnp.float32)
    real, imag = total[:half], total[half:]
    cart_ref[:half] = cosine * real - sine * imag
    cart_ref[half:] = sine * real + cosine * imag
    down = pltpu.make_async_remote_copy(
        src_ref=cart_ref,
        dst_ref=above_ref,
        send_sem=layer_send,
        recv_sem=layer_recv,
        device_id={"hgt": lax.max(layer - 1, 0)},
        device_id_type=MESH,
    )

    @pl.when(has_low)
    def _():
        down.start()

    @pl.when(has_high)
    def _():
        down.wait_recv()

    @pl.when(layer == layers - 1)
    def _():
        above_ref[...] = jnp.zeros_like(above_ref)

    for c in range(2):
        rows = slice(c * half, (c + 1) * half)
        blend = (1.0 - f2) * cart_ref[rows] + f2 * above_ref[rows]
        for row in range(tile_rows):
            for b in range(blocks):
                at = row * blocks + b
                out_ref[row, 0, c : c + 1, b * lanes_out : (b + 1) * lanes_out] = blend[at : at + 1]

    @pl.when(has_low)
    def _():
        down.wait_send()

    for copy in copies:
        copy.wait_send()


def body(
    polar_beams, band_start, band_weight, phase_rate, layer_wave, beam_map, range_map, pixel_frac
):
    count = lax.axis_size("sub")
    levels = band_start.shape[0]
    group = 2**levels
    beams, ranges = polar_beams.shape[2:]
    chunk = ranges // group
    pixel_rows, columns = beam_map.shape
    tile_rows = pixel_rows // count
    blocks = 16 // (2 * tile_rows)
    lanes_out = columns // blocks
    slots = chunk // SLOT
    width = group * beams
    margin = 2
    assert polar_beams.shape[0] == 1 and LANES * width // columns == 8
    vmem = pl.BlockSpec(memory_space=VMEM)
    smem = pl.BlockSpec(memory_space=pltpu.SMEM)

    x = pl.pallas_call(
        functools.partial(exchange_kernel, group),
        out_shape=jax.ShapeDtypeStruct((group, 2, beams, chunk), jnp.bfloat16),
        in_specs=[pl.BlockSpec(memory_space=pl.ANY)],
        out_specs=vmem,
        scratch_shapes=[
            pltpu.SemaphoreType.DMA((group,)),
            pltpu.SemaphoreType.DMA((group,)),
            pltpu.SemaphoreType.DMA,
        ],
        compiler_params=pltpu.CompilerParams(collective_id=0, has_side_effects=True),
    )(polar_beams)

    parts = pl.pallas_call(
        functools.partial(compute_kernel, levels, margin, float(ranges), tile_rows),
        out_shape=jax.ShapeDtypeStruct((count, 16, lanes_out), jnp.bfloat16),
        in_specs=[vmem, vmem, vmem, vmem, smem, vmem, vmem, vmem],
        out_specs=vmem,
        scratch_shapes=[
            VMEM((levels, 2 * width, width), jnp.bfloat16),
            VMEM((levels, 2, 2, beams, chunk), jnp.float32),
            VMEM((levels, 2, 2, beams, chunk), jnp.float32),
            VMEM((width, 2 * chunk), jnp.bfloat16),
            VMEM((2 * width, 2 * chunk), jnp.float32),
            VMEM((2, slots, 2, width + 16, SLOT), jnp.bfloat16),
            VMEM((2, slots, 2, width + 16, LANES), jnp.float32),
            VMEM((pixel_rows, 1, columns), jnp.float32),
            VMEM((pixel_rows, 1, columns), jnp.float32),
            VMEM((pixel_rows, 1, columns), jnp.int32),
            VMEM((pixel_rows, 1, columns), jnp.int32),
            VMEM((16, lanes_out), jnp.float32),
        ],
        compiler_params=pltpu.CompilerParams(vmem_limit_bytes=40 * 2**20),
    )(x, band_start, band_weight, phase_rate, layer_wave, beam_map, range_map, pixel_frac)

    return pl.pallas_call(
        functools.partial(finish_kernel, tile_rows),
        out_shape=jax.ShapeDtypeStruct((tile_rows, 1, 2, columns), jnp.float32),
        in_specs=[vmem, smem, vmem, vmem],
        out_specs=vmem,
        scratch_shapes=[
            VMEM((count, 16, lanes_out), jnp.bfloat16),
            VMEM((16, lanes_out), jnp.float32),
            VMEM((16, lanes_out), jnp.float32),
            VMEM((pixel_rows, 1, columns), jnp.int32),
            VMEM((pixel_rows, 1, columns), jnp.float32),
            VMEM((pixel_rows, 1, columns), jnp.float32),
            pltpu.SemaphoreType.DMA((count,)),
            pltpu.SemaphoreType.DMA((count,)),
            pltpu.SemaphoreType.DMA,
            pltpu.SemaphoreType.DMA,
        ],
        compiler_params=pltpu.CompilerParams(
            collective_id=1, has_side_effects=True, vmem_limit_bytes=40 * 2**20
        ),
    )(parts, layer_wave, range_map, pixel_frac)


def solution(mesh):
    in_specs = (P("hgt", None, "sub", None), P(), P(), P(), P("hgt"), P(), P(), P())
    out_specs = P("sub", "hgt", None, None)
    return jax.shard_map(body, mesh=mesh, in_specs=in_specs, out_specs=out_specs, check_vma=False)
```

```python
import functools

import jax
import jax.numpy as jnp
from jax import lax
from jax.experimental import pallas as pl
from jax.experimental.pallas import tpu as pltpu
from jax.sharding import PartitionSpec as P

range_phase = 0.003
LANES = 128
SLOT = 256
MESH = pl.DeviceIdType.MESH
VMEM = pltpu.VMEM


def sincos(x):
    q = jnp.floor(x * 0.6366197723675814 + 0.5)
    y = x - q * 1.5703125
    y = y - q * 4.837512969970703e-4
    y = y - q * 7.549789948768648e-8
    z = y * y
    s = y + y * z * (-1.6666654611e-1 + z * (8.3321608736e-3 + z * -1.9515295891e-4))
    c = 1.0 - 0.5 * z + z * z * (
        4.166664568298827e-2 + z * (-1.388731625493765e-3 + z * 2.443315711809948e-5)
    )
    n = q.astype(jnp.int32)
    odd = (n & 1) == 1
    sin_ = jnp.where(odd, c, s)
    cos_ = jnp.where(odd, s, c)
    sin_ = jnp.where((n & 2) == 2, -sin_, sin_)
    cos_ = jnp.where(((n + 1) & 2) == 2, -cos_, cos_)
    return sin_, cos_


def reverse_bits(value, width):
    result = 0
    for bit in range(width):
        result = result * 2 + ((value >> bit) & 1)
    return result


def iota(shape, dim):
    return lax.broadcasted_iota(jnp.int32, shape, dim)


def spread(out_ref, values):
    for y in range(values.shape[0]):
        out_ref[y] = values[y : y + 1].astype(out_ref.dtype)


def column_of(row, size):
    eye = iota((size, size), 0) == iota((size, size), 1)
    return jnp.sum(jnp.where(eye, row, 0.0), axis=1, keepdims=True)


def tables(levels, beams, first, total, wave, start_ref, weight_ref, rate_ref, m_ref, cos_ref, sin_ref):
    group = 2**levels
    width = group * beams
    chunk = cos_ref.shape[-1]
    lane = iota((beams, width), 1)
    lane_beam = (lane % beams).astype(jnp.float32)
    lane_sub = lane // beams
    taps = weight_ref.shape[3]
    eye = jnp.where(iota((beams, beams), 0) == iota((beams, beams), 1), 1.0, 0.0)
    weights = lax.dot_general(
        eye.astype(jnp.bfloat16),
        weight_ref[...].reshape(levels * 4 * taps, beams),
        (((1,), (1,)), ((), ())),
        preferred_element_type=jnp.float32,
    )
    pos = (iota((1, chunk), 1).astype(jnp.float32) + first + 0.5) / total
    for l in range(levels):
        for k in range(2):
            for h in range(2):
                start = column_of(start_ref[l, k, h : h + 1].astype(jnp.float32), beams)
                band = jnp.zeros((beams, width), jnp.float32)
                for t in range(taps):
                    at = ((l * 2 + k) * 2 + h) * taps + t
                    band = jnp.where(lane_beam == start + t, weights[:, at : at + 1], band)
                for s in range(group):
                    if (s >> l) & 1 == h:
                        child = (s & ~(1 << l)) | (k << l)
                        m_ref[l, pl.ds((k * group + s) * beams, beams), :] = jnp.where(
                            lane_sub == child, band, 0.0
                        ).astype(jnp.bfloat16)
                rate = column_of(rate_ref[l, k, h : h + 1], beams)
                sine, cosine = sincos(wave * rate * pos)
                cos_ref[l, k, h] = cosine
                sin_ref[l, k, h] = sine


def merge(levels, beams, x_ref, cur_ref, y_ref, m_ref, cos_ref, sin_ref):
    group = 2**levels
    width = group * beams
    chunk = x_ref.shape[-1]
    for s in range(group):
        for c in range(2):
            cur_ref[pl.ds(s * beams, beams), pl.ds(c * chunk, chunk)] = x_ref[s, c]
    for l in range(levels):
        y_ref[...] = jnp.dot(m_ref[l], cur_ref[...], preferred_element_type=jnp.float32)
        for s in range(group):
            h = (s >> l) & 1
            real = imag = 0.0
            for k in range(2):
                rows = pl.ds((k * group + s) * beams, beams)
                yr = y_ref[rows, pl.ds(0, chunk)]
                yi = y_ref[rows, pl.ds(chunk, chunk)]
                cosine, sine = cos_ref[l, k, h], sin_ref[l, k, h]
                real = real + (cosine * yr - sine * yi)
                imag = imag + (sine * yr + cosine * yi)
            cur_ref[pl.ds(s * beams, beams), pl.ds(0, chunk)] = real.astype(jnp.bfloat16)
            cur_ref[pl.ds(s * beams, beams), pl.ds(chunk, chunk)] = imag.astype(jnp.bfloat16)


def arrange(levels, beams, margin, cur_ref, l_ref, edge_ref):
    group = 2**levels
    width = group * beams
    chunk = cur_ref.shape[1] // 2
    padded = l_ref.shape[3]
    row = iota((padded, width), 0)
    lane = iota((padded, width), 1)
    beam = reverse_bits(lane // beams, levels) * beams + lane % beams
    for e in range(2):
        pick = jnp.where(row - (margin + 8 * e) == beam, 1.0, 0.0).astype(jnp.bfloat16)
        moved = jnp.dot(pick, cur_ref[...], preferred_element_type=jnp.float32)
        for m in range(l_ref.shape[1]):
            for c in range(2):
                part = moved[:, c * chunk + m * SLOT : c * chunk + (m + 1) * SLOT]
                l_ref[e, m, c] = part.astype(jnp.bfloat16)
                edge_ref[e, m, c] = jnp.broadcast_to(part[:, 0:1], (padded, LANES))


def pixels(margin, first, dest, tile_rows, range_ref, beam_ref, f0_ref, f1_ref, l_ref, edge_ref, part_ref):
    columns = range_ref.shape[2]
    slots = l_ref.shape[1]
    lanes_out = part_ref.shape[1]
    blocks = columns // lanes_out
    kappa = iota((SLOT, LANES), 0).astype(jnp.float32).astype(jnp.bfloat16)
    beta = iota((16, LANES), 0)
    for i in range(columns // LANES):
        e = i % 2
        top = 8 * i + 8 * e
        lhs = jnp.concatenate(
            [l_ref[e, m, c, top : top + 16] for m in range(slots) for c in range(2)], axis=0
        )
        edges = [
            jnp.concatenate([edge_ref[e, m, c, top : top + 16] for c in range(2)], axis=0)
            for m in range(slots)
        ]
        cols = slice(i * LANES, (i + 1) * LANES)
        ws, infos = [], []
        for row in range(tile_rows):
            y = dest * tile_rows + row
            u = range_ref[y, :, cols] - first
            f1 = f1_ref[y, :, cols]
            inside = (u >= 0) & (u < slots * SLOT)
            near = jnp.where(inside, u & (SLOT - 1), -8)
            near_b = near.astype(jnp.float32).astype(jnp.bfloat16)
            far_b = (near + 1).astype(jnp.float32).astype(jnp.bfloat16)
            w = jnp.where(
                kappa == near_b,
                (1.0 - f1).astype(jnp.bfloat16),
                jnp.where(kappa == far_b, f1.astype(jnp.bfloat16), jnp.bfloat16(0.0)),
            )
            ws.append(w)
            infos.append((u, f1, y))
        out = jnp.dot(lhs, jnp.concatenate(ws, axis=1), preferred_element_type=jnp.float32)
        for row in range(tile_rows):
            u, f1, y = infos[row]
            mine = out[:, row * LANES : (row + 1) * LANES]
            value = mine[0:32]
            for m in range(1, slots):
                value = jnp.where(u >= m * SLOT, mine[m * 32 : (m + 1) * 32], value)
            for m in range(slots):
                value = value + jnp.where(u == m * SLOT - 1, f1, 0.0) * edges[m]
            f0 = f0_ref[y, :, cols]
            low = beam_ref[y, :, cols] - (8 * i - margin)
            weight = jnp.where(beta == low, 1.0 - f0, jnp.where(beta == low + 1, f0, 0.0))
            lane0 = (i * LANES) % lanes_out
            for c in range(2):
                total = jnp.sum(value[c * 16 : c * 16 + 16] * weight, axis=0, keepdims=True)
                at = c * tile_rows * blocks + row * blocks + (i * LANES) // lanes_out
                part_ref[at : at + 1, lane0 : lane0 + LANES] = total


def far_first(step, count):
    return (count // 2 + (1 - 2 * (step % 2)) * ((step + 1) // 2)) % count


def kernel(
    levels, margin, tile_rows,
    polar_hbm, start_hbm, weight_hbm, rate_hbm, wave_hbm, beam_hbm, range_hbm, frac_hbm,
    out_ref,
    x_ref, start_ref, weight_ref, rate_ref, wave_ref, beam_ref, range_ref, frac_ref,
    m_ref, cos_ref, sin_ref, cur_ref, y_ref, l_ref, edge_ref,
    f0_ref, f1_ref, f2_ref, beam3_ref, range3_ref, part_ref, parts_ref, got_ref, cart_ref, above_ref,
    local_sem, x_send, x_recv, send_sem, recv_sem, layer_sem,
):
    me, layer = lax.axis_index("sub"), lax.axis_index("hgt")
    count, layers = lax.axis_size("sub"), lax.axis_size("hgt")
    group = 2**levels
    place = lax.rem(me, group)
    base = me - place
    beams, chunk = x_ref.shape[2:]
    total_ranges = float(polar_hbm.shape[-1])
    first = place * chunk
    lanes_out = part_ref.shape[1]
    blocks = range_ref.shape[1] // lanes_out
    half = tile_rows * blocks
    has_low, has_high = layer > 0, layer < layers - 1

    barrier = pltpu.get_barrier_semaphore()
    for i in range(1, count):
        pl.semaphore_signal(
            barrier, inc=1, device_id={"sub": lax.rem(me + i, count)}, device_id_type=MESH
        )

    @pl.when(has_low)
    def _():
        pl.semaphore_signal(barrier, inc=1, device_id={"hgt": layer - 1}, device_id_type=MESH)

    @pl.when(has_high)
    def _():
        pl.semaphore_signal(barrier, inc=1, device_id={"hgt": layer + 1}, device_id_type=MESH)

    def columns(index):
        return pl.ds(pl.multiple_of(index * chunk, chunk), chunk)

    pairs = [
        (wave_hbm, wave_ref), (rate_hbm, rate_ref), (start_hbm, start_ref),
        (weight_hbm, weight_ref), (frac_hbm, frac_ref), (beam_hbm, beam_ref),
        (range_hbm, range_ref), (polar_hbm.at[0, :, :, columns(place)], x_ref.at[place]),
    ]
    locals_ = [pltpu.make_async_copy(a, b, local_sem.at[n]) for n, (a, b) in enumerate(pairs)]
    for copy in locals_:
        copy.start()
    pl.semaphore_wait(barrier, count - 1 + has_low.astype(jnp.int32) + has_high.astype(jnp.int32))

    exchange = []
    for step in range(group - 1):
        i = far_first(step, group)
        there = lax.rem(place + i, group)
        exchange.append(
            pltpu.make_async_remote_copy(
                src_ref=polar_hbm.at[0, :, :, columns(there)],
                dst_ref=x_ref.at[place],
                send_sem=x_send.at[i],
                recv_sem=x_recv.at[i],
                device_id={"sub": base + there},
                device_id_type=MESH,
            )
        )
        exchange[-1].start()

    for copy in locals_:
        copy.wait()
    wave = wave_ref[0]
    tables(
        levels, beams, first.astype(jnp.float32), total_ranges, wave,
        start_ref, weight_ref, rate_ref, m_ref, cos_ref, sin_ref,
    )
    spread(f0_ref, frac_ref[0].astype(jnp.float32))
    spread(f1_ref, frac_ref[1].astype(jnp.float32))
    spread(f2_ref, frac_ref[2].astype(jnp.float32))
    spread(beam3_ref, beam_ref[...])
    spread(range3_ref, range_ref[...])

    def dense(ref):
        return jnp.concatenate(
            [
                ref[me * tile_rows + row, :, b * lanes_out : (b + 1) * lanes_out]
                for row in range(tile_rows)
                for b in range(blocks)
            ],
            axis=0,
        )

    angles = wave * range_phase * (dense(range3_ref).astype(jnp.float32) + dense(f1_ref))
    sine, cosine = sincos(angles)
    f2 = dense(f2_ref)

    for copy in exchange:
        copy.wait_recv()
    merge(levels, beams, x_ref, cur_ref, y_ref, m_ref, cos_ref, sin_ref)
    arrange(levels, beams, margin, cur_ref, l_ref, edge_ref)

    def to_owner(step, i):
        return pltpu.make_async_remote_copy(
            src_ref=parts_ref.at[step],
            dst_ref=got_ref.at[step],
            send_sem=send_sem.at[step],
            recv_sem=recv_sem.at[step],
            device_id={"sub": lax.rem(me + i, count)},
            device_id_type=MESH,
        )

    def one(step, carry):
        i = far_first(step, count)
        pixels(
            margin, first, lax.rem(me + i, count), tile_rows, range3_ref, beam3_ref, f0_ref, f1_ref,
            l_ref, edge_ref, part_ref,
        )
        parts_ref[step] = part_ref[...].astype(jnp.bfloat16)

        @pl.when(step < count - 1)
        def _():
            to_owner(step, i).start()

        return carry

    lax.fori_loop(0, count, one, 0)
    total = part_ref[...]
    for step in range(count - 1):
        to_owner(step, far_first(step, count)).wait_recv()
        total = total + got_ref[step].astype(jnp.float32)
    real, imag = total[:half], total[half:]
    cart_ref[:half] = cosine * real - sine * imag
    cart_ref[half:] = sine * real + cosine * imag
    down = pltpu.make_async_remote_copy(
        src_ref=cart_ref,
        dst_ref=above_ref,
        send_sem=layer_sem.at[0],
        recv_sem=layer_sem.at[1],
        device_id={"hgt": lax.max(layer - 1, 0)},
        device_id_type=MESH,
    )

    @pl.when(has_low)
    def _():
        down.start()

    @pl.when(has_high)
    def _():
        down.wait_recv()

    @pl.when(layer == layers - 1)
    def _():
        above_ref[...] = jnp.zeros_like(above_ref)

    for c in range(2):
        rows = slice(c * half, (c + 1) * half)
        blend = (1.0 - f2) * cart_ref[rows] + f2 * above_ref[rows]
        for row in range(tile_rows):
            for b in range(blocks):
                at = row * blocks + b
                out_ref[row, 0, c : c + 1, b * lanes_out : (b + 1) * lanes_out] = blend[at : at + 1]

    @pl.when(has_low)
    def _():
        down.wait_send()

    for copy in exchange:
        copy.wait_send()
    for step in range(count - 1):
        to_owner(step, far_first(step, count)).wait_send()


def body(
    polar_beams, band_start, band_weight, phase_rate, layer_wave, beam_map, range_map, pixel_frac
):
    count = lax.axis_size("sub")
    levels = band_start.shape[0]
    group = 2**levels
    beams, ranges = polar_beams.shape[2:]
    chunk = ranges // group
    pixel_rows, columns = beam_map.shape
    tile_rows = pixel_rows // count
    blocks = 16 // (2 * tile_rows)
    lanes_out = columns // blocks
    slots = chunk // SLOT
    width = group * beams
    assert polar_beams.shape[0] == 1 and LANES * width // columns == 8
    tap_rows = jnp.swapaxes(band_weight, 3, 4)
    small = [band_start, tap_rows, phase_rate]
    maps = [beam_map, range_map, pixel_frac]
    rows3 = (pixel_rows, 1, columns)
    dma = pltpu.SemaphoreType.DMA
    return pl.pallas_call(
        functools.partial(kernel, levels, 2, tile_rows),
        out_shape=jax.ShapeDtypeStruct((tile_rows, 1, 2, columns), jnp.float32),
        in_specs=[pl.BlockSpec(memory_space=pl.ANY)] * 8,
        out_specs=pl.BlockSpec(memory_space=VMEM),
        scratch_shapes=[
            VMEM((group, 2, beams, chunk), jnp.bfloat16),
            *[VMEM(a.shape, a.dtype) for a in small],
            pltpu.SMEM((1,), jnp.float32),
            *[VMEM(a.shape, a.dtype) for a in maps],
            VMEM((levels, 2 * width, width), jnp.bfloat16),
            VMEM((levels, 2, 2, beams, chunk), jnp.float32),
            VMEM((levels, 2, 2, beams, chunk), jnp.float32),
            VMEM((width, 2 * chunk), jnp.bfloat16),
            VMEM((2 * width, 2 * chunk), jnp.float32),
            VMEM((2, slots, 2, width + 16, SLOT), jnp.bfloat16),
            VMEM((2, slots, 2, width + 16, LANES), jnp.float32),
            VMEM(rows3, jnp.float32),
            VMEM(rows3, jnp.float32),
            VMEM(rows3, jnp.float32),
            VMEM(rows3, jnp.int32),
            VMEM(rows3, jnp.int32),
            VMEM((16, lanes_out), jnp.float32),
            VMEM((count, 16, lanes_out), jnp.bfloat16),
            VMEM((count, 16, lanes_out), jnp.bfloat16),
            VMEM((16, lanes_out), jnp.float32),
            VMEM((16, lanes_out), jnp.float32),
            dma((8,)),
            dma((group,)),
            dma((group,)),
            dma((count,)),
            dma((count,)),
            dma((2,)),
        ],
        compiler_params=pltpu.CompilerParams(
            collective_id=0, has_side_effects=True, vmem_limit_bytes=63 * 2**20 + 2**19
        ),
    )(
        polar_beams, band_start, tap_rows, phase_rate, layer_wave, beam_map, range_map, pixel_frac
    )


def solution(mesh):
    in_specs = (P("hgt", None, "sub", None), P(), P(), P(), P("hgt"), P(), P(), P())
    out_specs = P("sub", "hgt", None, None)
    return jax.shard_map(body, mesh=mesh, in_specs=in_specs, out_specs=out_specs, check_vma=False)
```

```python
import functools
import math

import jax
import jax.numpy as jnp
from jax import lax
from jax.experimental import pallas as pl
from jax.experimental.pallas import tpu as pltpu
from jax.sharding import PartitionSpec as P

range_phase = 0.003
LANES = 128
SLOT = 256
MESH = pl.DeviceIdType.MESH
VMEM = pltpu.VMEM


def sincos(x):
    q = jnp.floor(x * 0.6366197723675814 + 0.5)
    y = x - q * 1.5703125
    y = y - q * 4.837512969970703e-4
    y = y - q * 7.549789948768648e-8
    z = y * y
    s = y + y * z * (-1.6666654611e-1 + z * (8.3321608736e-3 + z * -1.9515295891e-4))
    c = 1.0 - 0.5 * z + z * z * (
        4.166664568298827e-2 + z * (-1.388731625493765e-3 + z * 2.443315711809948e-5)
    )
    n = q.astype(jnp.int32)
    odd = (n & 1) == 1
    sin_ = jnp.where(odd, c, s)
    cos_ = jnp.where(odd, s, c)
    sin_ = jnp.where((n & 2) == 2, -sin_, sin_)
    cos_ = jnp.where(((n + 1) & 2) == 2, -cos_, cos_)
    return sin_, cos_


def reverse_bits(value, width):
    result = 0
    for bit in range(width):
        result = result * 2 + ((value >> bit) & 1)
    return result


def iota(shape, dim):
    return lax.broadcasted_iota(jnp.int32, shape, dim)


def spread(out_ref, values):
    for y in range(values.shape[0]):
        out_ref[y] = values[y : y + 1].astype(out_ref.dtype)


def column_of(row, size):
    eye = iota((size, size), 0) == iota((size, size), 1)
    return jnp.sum(jnp.where(eye, row, 0.0), axis=1, keepdims=True)


def tables(levels, beams, first, total, wave, start_ref, weight_ref, rate_ref, m_ref, cos_ref, sin_ref):
    group = 2**levels
    width = group * beams
    chunk = cos_ref.shape[-1]
    lane = iota((beams, width), 1)
    lane_beam = (lane % beams).astype(jnp.float32)
    lane_sub = lane // beams
    taps = weight_ref.shape[3]
    eye = jnp.where(iota((beams, beams), 0) == iota((beams, beams), 1), 1.0, 0.0)
    weights = lax.dot_general(
        eye.astype(jnp.bfloat16),
        weight_ref[...].reshape(levels * 4 * taps, beams),
        (((1,), (1,)), ((), ())),
        preferred_element_type=jnp.float32,
    )
    pos = (iota((1, chunk), 1).astype(jnp.float32) + first + 0.5) / total
    for l in range(levels):
        for k in range(2):
            for h in range(2):
                start = column_of(start_ref[l, k, h : h + 1].astype(jnp.float32), beams)
                band = jnp.zeros((beams, width), jnp.float32)
                for t in range(taps):
                    at = ((l * 2 + k) * 2 + h) * taps + t
                    band = jnp.where(lane_beam == start + t, weights[:, at : at + 1], band)
                for s in range(group):
                    if (s >> l) & 1 == h:
                        child = (s & ~(1 << l)) | (k << l)
                        m_ref[l, pl.ds((k * group + s) * beams, beams), :] = jnp.where(
                            lane_sub == child, band, 0.0
                        ).astype(jnp.bfloat16)
                rate = column_of(rate_ref[l, k, h : h + 1], beams)
                sine, cosine = sincos(wave * rate * pos)
                cos_ref[l, k, h] = cosine
                sin_ref[l, k, h] = sine


def merge(levels, beams, x_ref, cur_ref, y_ref, m_ref, cos_ref, sin_ref):
    group = 2**levels
    width = group * beams
    chunk = x_ref.shape[-1]
    for s in range(group):
        for c in range(2):
            cur_ref[pl.ds(s * beams, beams), pl.ds(c * chunk, chunk)] = x_ref[s, c]
    for l in range(levels):
        y_ref[...] = jnp.dot(m_ref[l], cur_ref[...], preferred_element_type=jnp.float32)
        for s in range(group):
            h = (s >> l) & 1
            real = imag = 0.0
            for k in range(2):
                rows = pl.ds((k * group + s) * beams, beams)
                yr = y_ref[rows, pl.ds(0, chunk)]
                yi = y_ref[rows, pl.ds(chunk, chunk)]
                cosine, sine = cos_ref[l, k, h], sin_ref[l, k, h]
                real = real + (cosine * yr - sine * yi)
                imag = imag + (sine * yr + cosine * yi)
            cur_ref[pl.ds(s * beams, beams), pl.ds(0, chunk)] = real.astype(jnp.bfloat16)
            cur_ref[pl.ds(s * beams, beams), pl.ds(chunk, chunk)] = imag.astype(jnp.bfloat16)


def arrange(levels, beams, margin, cur_ref, l_ref, edge_ref):
    group = 2**levels
    width = group * beams
    chunk = cur_ref.shape[1] // 2
    padded = l_ref.shape[3]
    row = iota((padded, width), 0)
    lane = iota((padded, width), 1)
    beam = reverse_bits(lane // beams, levels) * beams + lane % beams
    for e in range(2):
        pick = jnp.where(row - (margin + 8 * e) == beam, 1.0, 0.0).astype(jnp.bfloat16)
        moved = jnp.dot(pick, cur_ref[...], preferred_element_type=jnp.float32)
        for m in range(l_ref.shape[1]):
            for c in range(2):
                part = moved[:, c * chunk + m * SLOT : c * chunk + (m + 1) * SLOT]
                l_ref[e, m, c] = part.astype(jnp.bfloat16)
                if m + 1 < l_ref.shape[1]:
                    edge_ref[e, m, c] = jnp.broadcast_to(part[:, SLOT - 1 :], (padded, LANES))


def near_sample(u, slots):
    near = u
    for m in range(1, slots):
        near = near - jnp.where(u >= m * SLOT - 1, SLOT, 0)
    return near


def interpolation(first, slots, i, y, range_ref, f1_ref):
    cols = slice(i * LANES, (i + 1) * LANES)
    kappa = iota((SLOT, LANES), 0).astype(jnp.float32).astype(jnp.bfloat16)
    near = near_sample(range_ref[y, :, cols] - first, slots)
    f1 = f1_ref[y, :, cols]
    near_b = near.astype(jnp.float32).astype(jnp.bfloat16)
    far_b = (near + 1).astype(jnp.float32).astype(jnp.bfloat16)
    return jnp.where(
        kappa == near_b,
        (1.0 - f1).astype(jnp.bfloat16),
        jnp.where(kappa == far_b, f1.astype(jnp.bfloat16), jnp.bfloat16(0.0)),
    )


def pixels(margin, first, dest, step, tile_rows, range_ref, beam_ref, f0_ref, f1_ref, l_ref, edge_ref, w_ref, part_ref):
    columns = range_ref.shape[2]
    slots = l_ref.shape[1]
    lanes_out = part_ref.shape[1]
    blocks = columns // lanes_out
    beta = iota((16, LANES), 0)
    for i in range(columns // LANES):
        e = i % 2
        top = 8 * i + 8 * e
        lhs = jnp.concatenate(
            [l_ref[e, m, c, top : top + 16] for m in range(slots) for c in range(2)], axis=0
        )
        edges = [
            jnp.concatenate([edge_ref[e, m, c, top : top + 16] for c in range(2)], axis=0)
            for m in range(slots - 1)
        ]
        cols = slice(i * LANES, (i + 1) * LANES)
        if w_ref is None:
            weights = jnp.concatenate(
                [
                    interpolation(first, slots, i, dest * tile_rows + row, range_ref, f1_ref)
                    for row in range(tile_rows)
                ],
                axis=1,
            )
        else:
            weights = w_ref[step, i]
        out = jnp.dot(lhs, weights, preferred_element_type=jnp.float32)
        for row in range(tile_rows):
            y = dest * tile_rows + row
            u = range_ref[y, :, cols] - first
            f1 = f1_ref[y, :, cols]
            mine = out[:, row * LANES : (row + 1) * LANES]
            value = mine[0:32]
            for m in range(1, slots):
                value = jnp.where(u >= m * SLOT - 1, mine[m * 32 : (m + 1) * 32], value)
            for m in range(1, slots):
                value = value + jnp.where(u == m * SLOT - 1, 1.0 - f1, 0.0) * edges[m - 1]
            f0 = f0_ref[y, :, cols]
            low = beam_ref[y, :, cols] - (8 * i - margin)
            weight = jnp.where(beta == low, 1.0 - f0, jnp.where(beta == low + 1, f0, 0.0))
            lane0 = (i * LANES) % lanes_out
            for c in range(2):
                total = jnp.sum(value[c * 16 : c * 16 + 16] * weight, axis=0, keepdims=True)
                at = c * tile_rows * blocks + row * blocks + (i * LANES) // lanes_out
                part_ref[at : at + 1, lane0 : lane0 + LANES] = total


def far_first(step, count):
    return (count // 2 + (1 - 2 * (step % 2)) * ((step + 1) // 2)) % count


def kernel(
    levels, margin, tile_rows, ahead,
    polar_hbm, start_hbm, weight_hbm, rate_hbm, wave_hbm, beam_hbm, range_hbm, frac_hbm,
    out_ref,
    x_ref, start_ref, weight_ref, rate_ref, wave_ref, beam_ref, range_ref, frac_ref,
    m_ref, cos_ref, sin_ref, cur_ref, y_ref, l_ref, edge_ref,
    f0_ref, f1_ref, f2_ref, beam3_ref, range3_ref, part_ref, parts_ref, got_ref, cart_ref, above_ref, w_ref,
    local_sem, x_send, x_recv, send_sem, recv_sem, layer_sem,
):
    me, layer = lax.axis_index("sub"), lax.axis_index("hgt")
    count, layers = lax.axis_size("sub"), lax.axis_size("hgt")
    group = 2**levels
    place = lax.rem(me, group)
    base = me - place
    beams, chunk = x_ref.shape[2:]
    total_ranges = float(polar_hbm.shape[-1])
    first = place * chunk
    lanes_out = part_ref.shape[1]
    blocks = range_ref.shape[1] // lanes_out
    half = tile_rows * blocks
    has_low, has_high = layer > 0, layer < layers - 1

    barrier = pltpu.get_barrier_semaphore()
    for i in range(1, count):
        pl.semaphore_signal(
            barrier, inc=1, device_id={"sub": lax.rem(me + i, count)}, device_id_type=MESH
        )

    @pl.when(has_low)
    def _():
        pl.semaphore_signal(barrier, inc=1, device_id={"hgt": layer - 1}, device_id_type=MESH)

    @pl.when(has_high)
    def _():
        pl.semaphore_signal(barrier, inc=1, device_id={"hgt": layer + 1}, device_id_type=MESH)

    def columns(index):
        return pl.ds(pl.multiple_of(index * chunk, chunk), chunk)

    pairs = [
        (wave_hbm, wave_ref), (rate_hbm, rate_ref), (start_hbm, start_ref),
        (weight_hbm, weight_ref), (frac_hbm, frac_ref), (beam_hbm, beam_ref),
        (range_hbm, range_ref), (polar_hbm.at[0, :, :, columns(place)], x_ref.at[place]),
    ]
    locals_ = [pltpu.make_async_copy(a, b, local_sem.at[n]) for n, (a, b) in enumerate(pairs)]
    for copy in locals_:
        copy.start()
    pl.semaphore_wait(barrier, count - 1 + has_low.astype(jnp.int32) + has_high.astype(jnp.int32))

    exchange = []
    for step in range(group - 1):
        i = far_first(step, group)
        there = lax.rem(place + i, group)
        exchange.append(
            pltpu.make_async_remote_copy(
                src_ref=polar_hbm.at[0, :, :, columns(there)],
                dst_ref=x_ref.at[place],
                send_sem=x_send.at[i],
                recv_sem=x_recv.at[i],
                device_id={"sub": base + there},
                device_id_type=MESH,
            )
        )
        exchange[-1].start()

    for copy in locals_:
        copy.wait()
    wave = wave_ref[0]
    tables(
        levels, beams, first.astype(jnp.float32), total_ranges, wave,
        start_ref, weight_ref, rate_ref, m_ref, cos_ref, sin_ref,
    )
    spread(f0_ref, frac_ref[0].astype(jnp.float32))
    spread(f1_ref, frac_ref[1].astype(jnp.float32))
    spread(f2_ref, frac_ref[2].astype(jnp.float32))
    spread(beam3_ref, beam_ref[...])
    spread(range3_ref, range_ref[...])

    def dense(ref):
        return jnp.concatenate(
            [
                ref[me * tile_rows + row, :, b * lanes_out : (b + 1) * lanes_out]
                for row in range(tile_rows)
                for b in range(blocks)
            ],
            axis=0,
        )

    angles = wave * range_phase * (dense(range3_ref).astype(jnp.float32) + dense(f1_ref))
    sine, cosine = sincos(angles)
    f2 = dense(f2_ref)

    def weights_of(step, carry):
        dest = lax.rem(me + far_first(step, count), count)
        for i in range(w_ref.shape[1]):
            for row in range(tile_rows):
                w_ref[step, i, :, row * LANES : (row + 1) * LANES] = interpolation(
                    first, l_ref.shape[1], i, dest * tile_rows + row, range3_ref, f1_ref
                )
        return carry

    if ahead:
        lax.fori_loop(0, count, weights_of, 0)
    for copy in exchange:
        copy.wait_recv()
    merge(levels, beams, x_ref, cur_ref, y_ref, m_ref, cos_ref, sin_ref)
    arrange(levels, beams, margin, cur_ref, l_ref, edge_ref)

    def to_owner(step, i):
        return pltpu.make_async_remote_copy(
            src_ref=parts_ref.at[step],
            dst_ref=got_ref.at[step],
            send_sem=send_sem.at[step],
            recv_sem=recv_sem.at[step],
            device_id={"sub": lax.rem(me + i, count)},
            device_id_type=MESH,
        )

    def one(step, carry):
        i = far_first(step, count)
        pixels(
            margin, first, lax.rem(me + i, count), step, tile_rows, range3_ref, beam3_ref, f0_ref,
            f1_ref, l_ref, edge_ref, w_ref if ahead else None, part_ref,
        )
        parts_ref[step] = part_ref[...].astype(jnp.bfloat16)

        @pl.when(step < count - 1)
        def _():
            to_owner(step, i).start()

        return carry

    lax.fori_loop(0, count, one, 0)
    total = part_ref[...]
    for step in range(count - 1):
        to_owner(step, far_first(step, count)).wait_recv()
        total = total + got_ref[step].astype(jnp.float32)
    real, imag = total[:half], total[half:]
    cart_ref[:half] = cosine * real - sine * imag
    cart_ref[half:] = sine * real + cosine * imag
    down = pltpu.make_async_remote_copy(
        src_ref=cart_ref,
        dst_ref=above_ref,
        send_sem=layer_sem.at[0],
        recv_sem=layer_sem.at[1],
        device_id={"hgt": lax.max(layer - 1, 0)},
        device_id_type=MESH,
    )

    @pl.when(has_low)
    def _():
        down.start()

    @pl.when(has_high)
    def _():
        down.wait_recv()

    @pl.when(layer == layers - 1)
    def _():
        above_ref[...] = jnp.zeros_like(above_ref)

    for c in range(2):
        rows = slice(c * half, (c + 1) * half)
        blend = (1.0 - f2) * cart_ref[rows] + f2 * above_ref[rows]
        for row in range(tile_rows):
            for b in range(blocks):
                at = row * blocks + b
                out_ref[row, 0, c : c + 1, b * lanes_out : (b + 1) * lanes_out] = blend[at : at + 1]

    @pl.when(has_low)
    def _():
        down.wait_send()

    for copy in exchange:
        copy.wait_send()
    for step in range(count - 1):
        to_owner(step, far_first(step, count)).wait_send()


def body(
    polar_beams, band_start, band_weight, phase_rate, layer_wave, beam_map, range_map, pixel_frac
):
    count = lax.axis_size("sub")
    levels = band_start.shape[0]
    group = 2**levels
    beams, ranges = polar_beams.shape[2:]
    chunk = ranges // group
    pixel_rows, columns = beam_map.shape
    tile_rows = pixel_rows // count
    blocks = 16 // (2 * tile_rows)
    lanes_out = columns // blocks
    slots = chunk // SLOT
    width = group * beams
    assert polar_beams.shape[0] == 1 and LANES * width // columns == 8
    tap_rows = jnp.swapaxes(band_weight, 3, 4)
    small = [band_start, tap_rows, phase_rate]
    maps = [beam_map, range_map, pixel_frac]
    rows3 = (pixel_rows, 1, columns)
    dma = pltpu.SemaphoreType.DMA
    w_shape = (count, columns // LANES, SLOT, tile_rows * LANES)
    ahead = 2 * math.prod(w_shape) <= 24 * 2**20
    if not ahead:
        w_shape = (1, 1, 16, LANES)
    return pl.pallas_call(
        functools.partial(kernel, levels, 2, tile_rows, ahead),
        out_shape=jax.ShapeDtypeStruct((tile_rows, 1, 2, columns), jnp.float32),
        in_specs=[pl.BlockSpec(memory_space=pl.ANY)] * 8,
        out_specs=pl.BlockSpec(memory_space=VMEM),
        scratch_shapes=[
            VMEM((group, 2, beams, chunk), jnp.bfloat16),
            *[VMEM(a.shape, a.dtype) for a in small],
            pltpu.SMEM((1,), jnp.float32),
            *[VMEM(a.shape, a.dtype) for a in maps],
            VMEM((levels, 2 * width, width), jnp.bfloat16),
            VMEM((levels, 2, 2, beams, chunk), jnp.float32),
            VMEM((levels, 2, 2, beams, chunk), jnp.float32),
            VMEM((width, 2 * chunk), jnp.bfloat16),
            VMEM((2 * width, 2 * chunk), jnp.float32),
            VMEM((2, slots, 2, width + 16, SLOT), jnp.bfloat16),
            VMEM((2, max(slots - 1, 1), 2, width + 16, LANES), jnp.float32),
            VMEM(rows3, jnp.float32),
            VMEM(rows3, jnp.float32),
            VMEM(rows3, jnp.float32),
            VMEM(rows3, jnp.int32),
            VMEM(rows3, jnp.int32),
            VMEM((16, lanes_out), jnp.float32),
            VMEM((count, 16, lanes_out), jnp.bfloat16),
            VMEM((count, 16, lanes_out), jnp.bfloat16),
            VMEM((16, lanes_out), jnp.float32),
            VMEM((16, lanes_out), jnp.float32),
            VMEM(w_shape, jnp.bfloat16),
            dma((8,)),
            dma((group,)),
            dma((group,)),
            dma((count,)),
            dma((count,)),
            dma((2,)),
        ],
        compiler_params=pltpu.CompilerParams(
            collective_id=0, has_side_effects=True, vmem_limit_bytes=254 * 2**18
        ),
    )(
        polar_beams, band_start, tap_rows, phase_rate, layer_wave, beam_map, range_map, pixel_frac
    )


def solution(mesh):
    in_specs = (P("hgt", None, "sub", None), P(), P(), P(), P("hgt"), P(), P(), P())
    out_specs = P("sub", "hgt", None, None)
    return jax.shard_map(body, mesh=mesh, in_specs=in_specs, out_specs=out_specs, check_vma=False)
```

```python
import functools
import math

import jax
import jax.numpy as jnp
from jax import lax
from jax.experimental import pallas as pl
from jax.experimental.pallas import tpu as pltpu
from jax.sharding import PartitionSpec as P

range_phase = 0.003
LANES = 128
SLOT = 256
MESH = pl.DeviceIdType.MESH
VMEM = pltpu.VMEM


def sincos(x):
    q = jnp.floor(x * 0.6366197723675814 + 0.5)
    y = x - q * 1.5703125
    y = y - q * 4.837512969970703e-4
    y = y - q * 7.549789948768648e-8
    z = y * y
    s = y + y * z * (-1.6666654611e-1 + z * (8.3321608736e-3 + z * -1.9515295891e-4))
    c = 1.0 - 0.5 * z + z * z * (
        4.166664568298827e-2 + z * (-1.388731625493765e-3 + z * 2.443315711809948e-5)
    )
    n = q.astype(jnp.int32)
    odd = (n & 1) == 1
    sin_ = jnp.where(odd, c, s)
    cos_ = jnp.where(odd, s, c)
    sin_ = jnp.where((n & 2) == 2, -sin_, sin_)
    cos_ = jnp.where(((n + 1) & 2) == 2, -cos_, cos_)
    return sin_, cos_


def reverse_bits(value, width):
    result = 0
    for bit in range(width):
        result = result * 2 + ((value >> bit) & 1)
    return result


def iota(shape, dim):
    return lax.broadcasted_iota(jnp.int32, shape, dim)


def spread(out_ref, values):
    for y in range(values.shape[0]):
        out_ref[y] = values[y : y + 1].astype(out_ref.dtype)


def column_of(row, size):
    eye = iota((size, size), 0) == iota((size, size), 1)
    return jnp.sum(jnp.where(eye, row, 0.0), axis=1, keepdims=True)


def tables(levels, beams, first, total, wave, start_ref, weight_ref, rate_ref, m_ref, cos_ref, sin_ref):
    group = 2**levels
    width = group * beams
    chunk = cos_ref.shape[-1]
    lane = iota((beams, width), 1)
    lane_beam = (lane % beams).astype(jnp.float32)
    lane_sub = lane // beams
    taps = weight_ref.shape[3]
    eye = jnp.where(iota((beams, beams), 0) == iota((beams, beams), 1), 1.0, 0.0)
    weights = lax.dot_general(
        eye.astype(jnp.bfloat16),
        weight_ref[...].reshape(levels * 4 * taps, beams),
        (((1,), (1,)), ((), ())),
        preferred_element_type=jnp.float32,
    )
    pos = (iota((1, chunk), 1).astype(jnp.float32) + first + 0.5) / total
    for l in range(levels):
        for k in range(2):
            for h in range(2):
                start = column_of(start_ref[l, k, h : h + 1].astype(jnp.float32), beams)
                band = jnp.zeros((beams, width), jnp.float32)
                for t in range(taps):
                    at = ((l * 2 + k) * 2 + h) * taps + t
                    band = jnp.where(lane_beam == start + t, weights[:, at : at + 1], band)
                for s in range(group):
                    if (s >> l) & 1 == h:
                        child = (s & ~(1 << l)) | (k << l)
                        m_ref[l, pl.ds((k * group + s) * beams, beams), :] = jnp.where(
                            lane_sub == child, band, 0.0
                        ).astype(jnp.bfloat16)
                rate = column_of(rate_ref[l, k, h : h + 1], beams)
                sine, cosine = sincos(wave * rate * pos)
                cos_ref[l, k, h] = cosine
                sin_ref[l, k, h] = sine


def merge(levels, beams, m, x_ref, cur_ref, y_ref, m_ref, cos_ref, sin_ref):
    group = 2**levels
    part = pl.ds(m * SLOT, SLOT)
    for s in range(group):
        for c in range(2):
            cur_ref[pl.ds(s * beams, beams), pl.ds(c * SLOT, SLOT)] = x_ref[s, c, :, part]
    for l in range(levels):
        y_ref[...] = jnp.dot(m_ref[l], cur_ref[...], preferred_element_type=jnp.float32)
        for s in range(group):
            h = (s >> l) & 1
            real = imag = 0.0
            for k in range(2):
                rows = pl.ds((k * group + s) * beams, beams)
                yr = y_ref[rows, pl.ds(0, SLOT)]
                yi = y_ref[rows, pl.ds(SLOT, SLOT)]
                cosine, sine = cos_ref[l, k, h, :, part], sin_ref[l, k, h, :, part]
                real = real + (cosine * yr - sine * yi)
                imag = imag + (sine * yr + cosine * yi)
            cur_ref[pl.ds(s * beams, beams), pl.ds(0, SLOT)] = real.astype(jnp.bfloat16)
            cur_ref[pl.ds(s * beams, beams), pl.ds(SLOT, SLOT)] = imag.astype(jnp.bfloat16)


def arrange(levels, beams, margin, m, cur_ref, l_ref, edge_ref):
    group = 2**levels
    width = group * beams
    padded = l_ref.shape[3]
    row = iota((padded, width), 0)
    lane = iota((padded, width), 1)
    beam = reverse_bits(lane // beams, levels) * beams + lane % beams
    for e in range(2):
        pick = jnp.where(row - (margin + 8 * e) == beam, 1.0, 0.0).astype(jnp.bfloat16)
        moved = jnp.dot(pick, cur_ref[...], preferred_element_type=jnp.float32)
        for c in range(2):
            part = moved[:, c * SLOT : (c + 1) * SLOT]
            l_ref[e, m, c] = part.astype(jnp.bfloat16)
            if m + 1 < l_ref.shape[1]:
                edge_ref[e, m, c] = jnp.broadcast_to(part[:, SLOT - 1 :], (padded, LANES))


def near_sample(u, slots):
    near = u
    for m in range(1, slots):
        near = near - jnp.where(u >= m * SLOT - 1, SLOT, 0)
    return near


def interpolation(first, slots, i, y, range_ref, f1_ref):
    cols = slice(i * LANES, (i + 1) * LANES)
    kappa = iota((SLOT, LANES), 0).astype(jnp.float32).astype(jnp.bfloat16)
    near = near_sample(range_ref[y, :, cols] - first, slots)
    f1 = f1_ref[y, :, cols]
    near_b = near.astype(jnp.float32).astype(jnp.bfloat16)
    far_b = (near + 1).astype(jnp.float32).astype(jnp.bfloat16)
    return jnp.where(
        kappa == near_b,
        (1.0 - f1).astype(jnp.bfloat16),
        jnp.where(kappa == far_b, f1.astype(jnp.bfloat16), jnp.bfloat16(0.0)),
    )


def beam_weights(margin, i, y, beam_ref, f0_ref):
    cols = slice(i * LANES, (i + 1) * LANES)
    beta = iota((16, LANES), 0)
    f0 = f0_ref[y, :, cols]
    low = beam_ref[y, :, cols] - (8 * i - margin)
    return jnp.where(beta == low, 1.0 - f0, jnp.where(beta == low + 1, f0, 0.0))


def pixels(
    margin, first, dest, step, tile_rows,
    range_ref, beam_ref, f0_ref, f1_ref, l_ref, edge_ref, w_ref, b_ref, part_ref,
):
    columns = range_ref.shape[2]
    slots = l_ref.shape[1]
    lanes_out = part_ref.shape[1]
    blocks = columns // lanes_out
    for i in range(columns // LANES):
        e = i % 2
        top = 8 * i + 8 * e
        lhs = jnp.concatenate(
            [l_ref[e, m, c, top : top + 16] for m in range(slots) for c in range(2)], axis=0
        )
        edges = [
            jnp.concatenate([edge_ref[e, m, c, top : top + 16] for c in range(2)], axis=0)
            for m in range(slots - 1)
        ]
        cols = slice(i * LANES, (i + 1) * LANES)
        if w_ref is None:
            weights = jnp.concatenate(
                [
                    interpolation(first, slots, i, dest * tile_rows + row, range_ref, f1_ref)
                    for row in range(tile_rows)
                ],
                axis=1,
            )
        else:
            weights = w_ref[step, i]
        out = jnp.dot(lhs, weights, preferred_element_type=jnp.float32)
        for row in range(tile_rows):
            y = dest * tile_rows + row
            u = range_ref[y, :, cols] - first
            f1 = f1_ref[y, :, cols]
            mine = out[:, row * LANES : (row + 1) * LANES]
            value = mine[0:32]
            for m in range(1, slots):
                value = jnp.where(u >= m * SLOT - 1, mine[m * 32 : (m + 1) * 32], value)
            for m in range(1, slots):
                value = value + jnp.where(u == m * SLOT - 1, 1.0 - f1, 0.0) * edges[m - 1]
            if w_ref is None:
                weight = beam_weights(margin, i, y, beam_ref, f0_ref)
            else:
                weight = b_ref[step, i, row]
            lane0 = (i * LANES) % lanes_out
            for c in range(2):
                total = jnp.sum(value[c * 16 : c * 16 + 16] * weight, axis=0, keepdims=True)
                at = c * tile_rows * blocks + row * blocks + (i * LANES) // lanes_out
                part_ref[at : at + 1, lane0 : lane0 + LANES] = total


def far_first(step, count):
    return (count // 2 + (1 - 2 * (step % 2)) * ((step + 1) // 2)) % count


def kernel(
    levels, margin, tile_rows, ahead,
    polar_hbm, start_hbm, weight_hbm, rate_hbm, wave_hbm, beam_hbm, range_hbm, frac_hbm,
    out_ref,
    x_ref, start_ref, weight_ref, rate_ref, wave_ref, beam_ref, range_ref, frac_ref,
    m_ref, cos_ref, sin_ref, cur_ref, y_ref, l_ref, edge_ref,
    f0_ref, f1_ref, f2_ref, beam3_ref, range3_ref, part_ref, parts_ref, got_ref, cart_ref, above_ref, w_ref, b_ref,
    local_sem, x_send, x_recv, send_sem, recv_sem, layer_sem,
):
    me, layer = lax.axis_index("sub"), lax.axis_index("hgt")
    count, layers = lax.axis_size("sub"), lax.axis_size("hgt")
    group = 2**levels
    place = lax.rem(me, group)
    base = me - place
    beams, chunk = x_ref.shape[2:]
    total_ranges = float(polar_hbm.shape[-1])
    first = place * chunk
    lanes_out = part_ref.shape[1]
    blocks = range_ref.shape[1] // lanes_out
    half = tile_rows * blocks
    has_low, has_high = layer > 0, layer < layers - 1

    barrier = pltpu.get_barrier_semaphore()
    for i in range(1, count):
        pl.semaphore_signal(
            barrier, inc=1, device_id={"sub": lax.rem(me + i, count)}, device_id_type=MESH
        )

    @pl.when(has_low)
    def _():
        pl.semaphore_signal(barrier, inc=1, device_id={"hgt": layer - 1}, device_id_type=MESH)

    @pl.when(has_high)
    def _():
        pl.semaphore_signal(barrier, inc=1, device_id={"hgt": layer + 1}, device_id_type=MESH)

    def columns(index):
        return pl.ds(pl.multiple_of(index * chunk, chunk), chunk)

    pairs = [
        (wave_hbm, wave_ref), (rate_hbm, rate_ref), (start_hbm, start_ref),
        (weight_hbm, weight_ref), (frac_hbm, frac_ref), (beam_hbm, beam_ref),
        (range_hbm, range_ref), (polar_hbm.at[0, :, :, columns(place)], x_ref.at[place]),
    ]
    locals_ = [pltpu.make_async_copy(a, b, local_sem.at[n]) for n, (a, b) in enumerate(pairs)]
    for copy in locals_:
        copy.start()
    pl.semaphore_wait(barrier, count - 1 + has_low.astype(jnp.int32) + has_high.astype(jnp.int32))

    slots = l_ref.shape[1]
    exchange = []
    for m in range(slots):
        exchange.append([])
        for step in range(group - 1):
            i = far_first(step, group)
            there = lax.rem(place + i, group)
            source = pl.ds(pl.multiple_of(there * chunk + m * SLOT, SLOT), SLOT)
            copy = pltpu.make_async_remote_copy(
                src_ref=polar_hbm.at[0, :, :, source],
                dst_ref=x_ref.at[place, :, :, pl.ds(m * SLOT, SLOT)],
                send_sem=x_send.at[m, i],
                recv_sem=x_recv.at[m, i],
                device_id={"sub": base + there},
                device_id_type=MESH,
            )
            exchange[m].append(copy)
            copy.start()

    for copy in locals_:
        copy.wait()
    wave = wave_ref[0]
    tables(
        levels, beams, first.astype(jnp.float32), total_ranges, wave,
        start_ref, weight_ref, rate_ref, m_ref, cos_ref, sin_ref,
    )
    spread(f0_ref, frac_ref[0].astype(jnp.float32))
    spread(f1_ref, frac_ref[1].astype(jnp.float32))
    spread(f2_ref, frac_ref[2].astype(jnp.float32))
    spread(beam3_ref, beam_ref[...])
    spread(range3_ref, range_ref[...])

    def dense(ref):
        return jnp.concatenate(
            [
                ref[me * tile_rows + row, :, b * lanes_out : (b + 1) * lanes_out]
                for row in range(tile_rows)
                for b in range(blocks)
            ],
            axis=0,
        )

    angles = wave * range_phase * (dense(range3_ref).astype(jnp.float32) + dense(f1_ref))
    sine, cosine = sincos(angles)
    f2 = dense(f2_ref)

    def weights_of(step, carry):
        dest = lax.rem(me + far_first(step, count), count)
        for i in range(w_ref.shape[1]):
            for row in range(tile_rows):
                w_ref[step, i, :, row * LANES : (row + 1) * LANES] = interpolation(
                    first, slots, i, dest * tile_rows + row, range3_ref, f1_ref
                )
                b_ref[step, i, row] = beam_weights(
                    margin, i, dest * tile_rows + row, beam3_ref, f0_ref
                )
        return carry

    if ahead:
        lax.fori_loop(0, count, weights_of, 0)
    for m in range(slots):
        for copy in exchange[m]:
            copy.wait_recv()
        merge(levels, beams, m, x_ref, cur_ref, y_ref, m_ref, cos_ref, sin_ref)
        arrange(levels, beams, margin, m, cur_ref, l_ref, edge_ref)

    def to_owner(step, i):
        return pltpu.make_async_remote_copy(
            src_ref=parts_ref.at[step],
            dst_ref=got_ref.at[step],
            send_sem=send_sem.at[step],
            recv_sem=recv_sem.at[step],
            device_id={"sub": lax.rem(me + i, count)},
            device_id_type=MESH,
        )

    def one(step, carry):
        i = far_first(step, count)
        pixels(
            margin, first, lax.rem(me + i, count), step, tile_rows, range3_ref, beam3_ref, f0_ref,
            f1_ref, l_ref, edge_ref, w_ref if ahead else None, b_ref, part_ref,
        )
        parts_ref[step] = part_ref[...].astype(jnp.bfloat16)

        @pl.when(step < count - 1)
        def _():
            to_owner(step, i).start()

        return carry

    lax.fori_loop(0, count, one, 0)
    total = part_ref[...]
    for step in range(count - 1):
        to_owner(step, far_first(step, count)).wait_recv()
        total = total + got_ref[step].astype(jnp.float32)
    real, imag = total[:half], total[half:]
    cart_ref[:half] = cosine * real - sine * imag
    cart_ref[half:] = sine * real + cosine * imag
    down = pltpu.make_async_remote_copy(
        src_ref=cart_ref,
        dst_ref=above_ref,
        send_sem=layer_sem.at[0],
        recv_sem=layer_sem.at[1],
        device_id={"hgt": lax.max(layer - 1, 0)},
        device_id_type=MESH,
    )

    @pl.when(has_low)
    def _():
        down.start()

    @pl.when(has_high)
    def _():
        down.wait_recv()

    @pl.when(layer == layers - 1)
    def _():
        above_ref[...] = jnp.zeros_like(above_ref)

    for c in range(2):
        rows = slice(c * half, (c + 1) * half)
        blend = (1.0 - f2) * cart_ref[rows] + f2 * above_ref[rows]
        for row in range(tile_rows):
            for b in range(blocks):
                at = row * blocks + b
                out_ref[row, 0, c : c + 1, b * lanes_out : (b + 1) * lanes_out] = blend[at : at + 1]

    @pl.when(has_low)
    def _():
        down.wait_send()

    for copies in exchange:
        for copy in copies:
            copy.wait_send()
    for step in range(count - 1):
        to_owner(step, far_first(step, count)).wait_send()


def body(
    polar_beams, band_start, band_weight, phase_rate, layer_wave, beam_map, range_map, pixel_frac
):
    count = lax.axis_size("sub")
    levels = band_start.shape[0]
    group = 2**levels
    beams, ranges = polar_beams.shape[2:]
    chunk = ranges // group
    pixel_rows, columns = beam_map.shape
    tile_rows = pixel_rows // count
    blocks = 16 // (2 * tile_rows)
    lanes_out = columns // blocks
    slots = chunk // SLOT
    width = group * beams
    assert polar_beams.shape[0] == 1 and LANES * width // columns == 8
    tap_rows = jnp.swapaxes(band_weight, 3, 4)
    small = [band_start, tap_rows, phase_rate]
    maps = [beam_map, range_map, pixel_frac]
    rows3 = (pixel_rows, 1, columns)
    dma = pltpu.SemaphoreType.DMA
    w_shape = (count, columns // LANES, SLOT, tile_rows * LANES)
    ahead = 2 * math.prod(w_shape) <= 24 * 2**20
    b_shape = (*w_shape[:2], tile_rows, 16, LANES)
    if not ahead:
        w_shape, b_shape = (1, 1, 16, LANES), (1, 1, 1, 16, LANES)
    return pl.pallas_call(
        functools.partial(kernel, levels, 2, tile_rows, ahead),
        out_shape=jax.ShapeDtypeStruct((tile_rows, 1, 2, columns), jnp.float32),
        in_specs=[pl.BlockSpec(memory_space=pl.ANY)] * 8,
        out_specs=pl.BlockSpec(memory_space=VMEM),
        scratch_shapes=[
            VMEM((group, 2, beams, chunk), jnp.bfloat16),
            *[VMEM(a.shape, a.dtype) for a in small],
            pltpu.SMEM((1,), jnp.float32),
            *[VMEM(a.shape, a.dtype) for a in maps],
            VMEM((levels, 2 * width, width), jnp.bfloat16),
            VMEM((levels, 2, 2, beams, chunk), jnp.float32),
            VMEM((levels, 2, 2, beams, chunk), jnp.float32),
            VMEM((width, 2 * SLOT), jnp.bfloat16),
            VMEM((2 * width, 2 * SLOT), jnp.float32),
            VMEM((2, slots, 2, width + 16, SLOT), jnp.bfloat16),
            VMEM((2, max(slots - 1, 1), 2, width + 16, LANES), jnp.float32),
            VMEM(rows3, jnp.float32),
            VMEM(rows3, jnp.float32),
            VMEM(rows3, jnp.float32),
            VMEM(rows3, jnp.int32),
            VMEM(rows3, jnp.int32),
            VMEM((16, lanes_out), jnp.float32),
            VMEM((count, 16, lanes_out), jnp.bfloat16),
            VMEM((count, 16, lanes_out), jnp.bfloat16),
            VMEM((16, lanes_out), jnp.float32),
            VMEM((16, lanes_out), jnp.float32),
            VMEM(w_shape, jnp.bfloat16),
            VMEM(b_shape, jnp.float32),
            dma((8,)),
            dma((slots, group)),
            dma((slots, group)),
            dma((count,)),
            dma((count,)),
            dma((2,)),
        ],
        compiler_params=pltpu.CompilerParams(
            collective_id=0, has_side_effects=True, vmem_limit_bytes=63 * 2**20 + 2**19
        ),
    )(
        polar_beams, band_start, tap_rows, phase_rate, layer_wave, beam_map, range_map, pixel_frac
    )


def solution(mesh):
    in_specs = (P("hgt", None, "sub", None), P(), P(), P(), P("hgt"), P(), P(), P())
    out_specs = P("sub", "hgt", None, None)
    return jax.shard_map(body, mesh=mesh, in_specs=in_specs, out_specs=out_specs, check_vma=False)
```
